32 devices in a mesh: samp: 8 (over z, y), col: 4 (over x, core).
Axes of the slice: x: 2, y: 2, z: 4, core: 2. Of those that a mesh axis runs over, the one named last changes fastest.
Arguments:
- spectra: float32 [16384, 8192], P('samp', 'col'), as said below
- w_start: float32 [16384, 512], P('samp'), may hold values from 0.05 to 1
- h_start: float32 [8192, 512], P('col'), may hold values from 0.05 to 1
Outputs:
- w_factor: float32 [16384, 512], P('samp')
- h_factor: float32 [8192, 512], P('col')
The draws below stay inside these ranges and needn't reach their ends.
Inputs may be any that keep to these rules, and one draw needn't show every extreme that they name: `spectra`: every entry is positive.
All inputs are finite; a program needn't handle non-finite values.
Results may differ from the reference program's by a relative error of at most 0.0003.
Values sent between devices are 32-bit elements; how exact they have to be, the bound alone decides.
A program may use at most 128 MiB of HBM per device.

```python
import math
import jax
import jax.numpy as jnp
from jax import lax

K = 512
N = 8192
BLOCK = 128
SWEEPS = 3
M = 16384


def draw_spectra(key, part):
    key_rows, key_cols, key_cells = jax.random.split(key, 3)
    row_scale = jnp.exp(jax.random.uniform(key_rows, (M, 1), jnp.float32, math.log(0.3), math.log(3.0)))
    col_scale = jnp.exp(jax.random.uniform(key_cols, (1, N), jnp.float32, math.log(0.3), math.log(3.0)))
    cells = jnp.exp(jax.random.uniform(key_cells, (M, N), jnp.float32, math.log(0.5), math.log(2.0)))
    return (64.0 * row_scale * col_scale * cells).astype(jnp.float32)


def block_scale(rng, extent, cuts, low, high):
    def one(axis_at, parts):
        draws = jax.random.uniform(jax.random.fold_in(jax.random.fold_in(rng, 6), axis_at), (parts,), jnp.float32, low / len(cuts), high / len(cuts))
        return jnp.repeat(jnp.exp(draws), extent[axis_at] // parts).reshape((-1,) + (1,) * (len(extent) - axis_at - 1))

    loudness = one(*cuts[0])
    for cut in cuts[1:]:
        loudness = loudness * one(*cut)
    return loudness


def setup_inputs(seed: int = 0) -> dict:
    streams_of = jax.random.split(jax.random.key(seed), 4)
    spectra = draw_spectra(jax.random.fold_in(streams_of[3], 71), 0)
    w_start = jnp.clip(0.05 + 0.95 * jax.random.uniform(streams_of[1], (M, K), jnp.float32) ** block_scale(streams_of[1], (M, K), ((0, 8),), -0.2, 0.2), 0.05, 1.0)
    h_start = jnp.clip(0.05 + 0.95 * jax.random.uniform(streams_of[2], (N, K), jnp.float32) ** block_scale(streams_of[2], (N, K), ((0, 4),), -0.2, 0.2), 0.05, 1.0)
    return dict(spectra=spectra, w_start=w_start, h_start=h_start)


floor_value = 1e-6


def sweep_factor(factor, product, gram_matrix):
    rank_width = gram_matrix.shape[0]
    for sweep_index in range(SWEEPS):
        for offset in range(0, rank_width, BLOCK):
            gram_cols = gram_matrix[:, offset:offset + BLOCK]
            majorant = jnp.sum(gram_matrix[offset:offset + BLOCK, offset:offset + BLOCK], axis=1)
            update = product[:, offset:offset + BLOCK] - jnp.dot(factor, gram_cols, precision=lax.Precision.HIGHEST, preferred_element_type=jnp.float32)
            new_block = jnp.maximum(factor[:, offset:offset + BLOCK] + update / majorant, floor_value)
            factor = lax.dynamic_update_slice_in_dim(factor, new_block, offset, 1)
    return factor


def contract_rows(left, right):
    return lax.dot_general(left, right, (((0,), (0,)), ((), ())), precision=lax.Precision.HIGHEST, preferred_element_type=jnp.float32)


def reference(spectra, w_start, h_start):
    prod_w = jnp.dot(spectra, h_start, precision=lax.Precision.HIGHEST, preferred_element_type=jnp.float32)
    gram_h = contract_rows(h_start, h_start)
    w_factor = sweep_factor(w_start, prod_w, gram_h)
    prod_h = contract_rows(spectra, w_factor)
    gram_w = contract_rows(w_factor, w_factor)
    h_factor = sweep_factor(h_start, prod_h, gram_w)
    return w_factor, h_factor
```

```python
import functools

import jax
import jax.numpy as jnp
from jax import lax
from jax.experimental import pallas as pl
from jax.experimental.pallas import tpu as pltpu
from jax.sharding import PartitionSpec as P

BLOCK = 128
SWEEPS = 3
FLOOR = 1e-06
MESH = pl.DeviceIdType.MESH
F32 = jnp.float32
BF16 = jnp.bfloat16
CORES = 2
DEPTH = 4
PIECES = 4
TILE = 256


def split(x):
    high = x.astype(BF16)
    return high, (x - high.astype(F32)).astype(BF16)


def dot(a, b):
    return jnp.dot(a, b, preferred_element_type=F32)


def dot3(ah, al, bh, bl):
    return dot(ah, bh) + (dot(ah, bl) + dot(al, bh))


def kernel(
    n_samp, n_col, spectra, w_start, h_start, w_out, h_out,
    spec, w_full, h_full, hh, hl, wth, wtl, pt, prod, acc, xrecv, ring_a, ring_b,
    gp, gcore, gring_a, gring_b, gx, gram, gcat, fh, fl,
    load_sem, core_sem, x_sem, ag_sem, fwd_sem, ring_sem, back_sem,
    gcore_sem, gring_sem, gx_sem, gback_sem, gout_sem, out_sem,
):
    rows, rank = w_full.shape
    cols = h_full.shape[0]
    chips = n_col // CORES
    rb = rows // n_col
    qb = cols // n_samp
    half_rank = rank // 2
    gb = half_rank // n_samp

    samp = lax.axis_index("samp")
    col = lax.axis_index("col")
    core = lax.rem(col, CORES)
    chip = col // CORES
    mate = {"col": chip * CORES + 1 - core}
    x_right = {"col": lax.rem(chip + 1, chips) * CORES + core}
    x_left = {"col": lax.rem(chip + chips - 1, chips) * CORES + core}
    width = n_samp // DEPTH
    z, y = samp // width, lax.rem(samp, width)
    pos = y * DEPTH + z + lax.rem(y, 2) * (DEPTH - 1 - 2 * z)

    def member(p):
        p = lax.rem(p + 2 * n_samp, n_samp)
        py, pr = p // DEPTH, lax.rem(p, DEPTH)
        pz = pr + lax.rem(py, 2) * (DEPTH - 1 - 2 * pr)
        return pz * width + py

    ring_next = {"samp": member(pos + 1)}
    ring_prev = {"samp": member(pos - 1)}

    def rows_at(start, size):
        return pl.ds(pl.multiple_of(start, size), size)

    def remote(src, dst, sems, index, device):
        return pltpu.make_async_remote_copy(
            src_ref=src, dst_ref=dst, send_sem=sems.at[(0,) + index], recv_sem=sems.at[(1,) + index],
            device_id=device, device_id_type=MESH,
        )

    sent = []

    def send(*args):
        copy = remote(*args)
        copy.start()
        sent.append(copy)
        return copy

    h_load = pltpu.make_async_copy(h_start, h_full, load_sem.at[0])
    h_load.start()
    order = []
    for t in range(chips):
        dest = lax.rem(chip - 1 - t + 2 * chips, chips)
        order.append((dest, dest * CORES + 1 - core, dest * CORES + core))
    spec_loads = []
    for t, (_, first, second) in enumerate(order):
        for u, blk in enumerate((first, second)):
            copy = pltpu.make_async_copy(
                spectra.at[rows_at(blk * rb, rb)], spec.at[rows_at(blk * rb, rb)], load_sem.at[2 + 2 * t + u]
            )
            copy.start()
            spec_loads.append(copy)
    own_w = rows_at(col * rb, rb)
    w_load = pltpu.make_async_copy(w_start.at[own_w], w_full.at[own_w], load_sem.at[1])
    w_load.start()

    barrier = pltpu.get_barrier_semaphore()
    greet = [mate, x_right, x_left, ring_next, ring_prev]
    for device in greet:
        pl.semaphore_signal(barrier, inc=1, device_id=device, device_id_type=MESH)
    pl.semaphore_wait(barrier, len(greet))

    def ring_reduce(data, base, block, recv_a, recv_b, sems):
        part = block // 2
        last = None
        for t in range(n_samp):
            current = []
            for way, (recv, device, sign) in enumerate(((recv_a, ring_next, 1), (recv_b, ring_prev, -1))):
                owner = member(pos - sign * (1 + t))
                where = rows_at(base + owner * block + way * part, part)
                if t > 0:
                    last[way].wait_recv()
                    data[where] += recv[t - 1]
                if t < n_samp - 1:
                    current.append(send(data.at[where], recv.at[t], sems, (way, t), device))
            last = current
            yield

    def ring_gather(data, base, block, sems):
        part = block // 2
        last = None
        for t in range(n_samp):
            current = []
            for way, (device, sign) in enumerate(((ring_next, 1), (ring_prev, -1))):
                owner = member(pos - sign * t)
                where = rows_at(base + owner * block + way * part, part)
                if t > 0:
                    last[way].wait_recv()
                if t < n_samp - 1:
                    current.append(send(data.at[where], data.at[where], sems, (way, t), device))
            last = current
            yield

    def gram_sum(i):
        mine = core * half_rank
        other = (1 - core) * half_rank
        copy = send(gp.at[i, rows_at(other, half_rank)], gcore.at[i], gcore_sem, (i,), mate)
        yield
        copy.wait_recv()
        gp[i, rows_at(mine, half_rank)] += gcore[i]
        yield from ring_reduce(gp.at[i], mine, gb, gring_a.at[i], gring_b.at[i], gring_sem.at[:, i])
        own = rows_at(mine + samp * gb, gb)
        total = gp[i, own]
        for t in range(chips - 1):
            source = gp.at[i, own] if t == 0 else gx.at[i, t - 1]
            copy = send(source, gx.at[i, t], gx_sem, (i, t), x_right)
            yield
            copy.wait_recv()
            total = total + gx[i, t]
        gram[i, own] = total
        yield from ring_gather(gram.at[i], mine, gb, gback_sem.at[:, i])
        where = rows_at(mine, half_rank)
        copy = send(gram.at[i, where], gram.at[i, where], gout_sem, (i,), mate)
        yield
        copy.wait_recv()

    def sweep(factor, product, g):
        n = factor.shape[0]
        scale = []
        for b in range(rank // BLOCK):
            cols_b = slice(b * BLOCK, (b + 1) * BLOCK)
            high, low = split(gram[g, :, cols_b])
            gcat[b, :, :BLOCK] = high
            gcat[b, :, BLOCK:] = low
            scale.append(1.0 / jnp.sum(gram[g, cols_b, cols_b], axis=0, keepdims=True))
            high, low = split(factor[:, cols_b])
            fh[:n, cols_b] = high
            fl[:n, cols_b] = low

        def one(_, carry):
            for b in range(rank // BLOCK):
                cols_b = slice(b * BLOCK, (b + 1) * BLOCK)
                both = dot(fh[:n], gcat[b])
                low = dot(fl[:n], gcat[b, :, :BLOCK])
                fg = both[:, :BLOCK] + (both[:, BLOCK:] + low)
                block = jnp.maximum(factor[:, cols_b] + (product[:, cols_b] - fg) * scale[b], FLOOR)
                factor[:, cols_b] = block
                high, low = split(block)
                fh[:n, cols_b] = high
                fl[:n, cols_b] = low
            return carry

        lax.fori_loop(0, SWEEPS, one, 0)

    h_load.wait()
    share = h_full[rows_at(samp * qb, qb)]
    th, tl = split(share.T)
    bh, bl = split(share)
    gp[0] = dot3(th, tl, bh, bl)
    gram_h = gram_sum(0)
    next(gram_h)

    def split_h(i, carry):
        where = rows_at(i * TILE, TILE)
        hh[where], hl[where] = split(h_full[where])
        return carry

    lax.fori_loop(0, cols // TILE, split_h, 0)

    def product_block(blk, store):
        tile = min(TILE, rb)

        def body(i, carry):
            sh, sl = split(spec[rows_at(blk * rb + i * tile, tile)])
            store[rows_at(i * tile, tile)] = dot3(sh, sl, hh[...], hl[...])
            return carry

        lax.fori_loop(0, rb // tile, body, 0)

    x_copy = None
    for t, (_, first, second) in enumerate(order):
        outgoing = prod.at[pl.ds(t * rb, rb)]
        incoming = prod.at[pl.ds((chips + t) * rb, rb)]
        spec_loads[2 * t].wait()
        product_block(first, outgoing)
        core_copy = send(outgoing, incoming, core_sem, (t,), mate)
        next(gram_h)
        spec_loads[2 * t + 1].wait()
        product_block(second, acc.at[t])
        core_copy.wait_recv()
        acc[t] += incoming[...]
        if t < chips - 1:
            if t > 0:
                x_copy.wait_recv()
                acc[t] += xrecv[t - 1]
            x_copy = send(acc.at[t], xrecv.at[t], x_sem, (t,), x_right)
        next(gram_h)
    for _ in gram_h:
        pass
    x_copy.wait_recv()
    acc[chips - 1] += xrecv[chips - 2]

    w_load.wait()
    sweep(w_full.at[own_w], acc.at[chips - 1], 0)

    for copy in sent:
        copy.wait_send()
    sent.clear()
    piece = rb // PIECES

    def w_piece(block, q):
        return w_full.at[rows_at(block * rb + q * piece, piece)]

    x_arrivals = [send(w_piece(col, q), w_piece(col, q), ag_sem, (0, q), x_right) for q in range(PIECES)]
    mate_arrivals = [send(w_piece(col, q), w_piece(col, q), fwd_sem, (0, q), mate) for q in range(PIECES)]

    def transpose_into(t, block, half):
        step = min(TILE, rb)
        for i in range(rb // step):
            high, low = split(w_full[rows_at(block * rb + i * step, step)].T)
            where = rows_at(half * rb + i * step, step)
            wth[t, :, where] = high
            wtl[t, :, where] = low

    transpose_into(0, col, core)
    lanes = rows_at(core * rb, rb)
    bh, bl = split(w_full[own_w])
    gp[1] = dot3(wth[0, :, lanes], wtl[0, :, lanes], bh, bl)
    gram_w = gram_sum(1)
    next(gram_w)
    for copy in mate_arrivals:
        copy.wait_recv()
    transpose_into(0, chip * CORES + 1 - core, 1 - core)
    next(gram_w)

    def product_tiles(t, source):
        span = CORES * rb

        def body(i, carry):
            lane = rows_at(i * TILE, TILE)
            sh, sl = split(spec[rows_at(source * span, span), lane])
            part = dot3(wth[t], wtl[t], sh, sl)
            if t > 0:
                part = part + pt[:, lane]
            if t == chips - 1:
                prod[lane] = part.T
            else:
                pt[:, lane] = part
            return carry

        lax.fori_loop(0, cols // TILE, body, 0)

    product_tiles(0, chip)
    for t in range(1, chips):
        source = lax.rem(chip - t + chips, chips)
        same = source * CORES + core
        later, mate_copies = [], []
        for q in range(PIECES):
            x_arrivals[q].wait_recv()
            if t < chips - 1:
                later.append(send(w_piece(same, q), w_piece(same, q), ag_sem, (t, q), x_right))
            mate_copies.append(send(w_piece(same, q), w_piece(same, q), fwd_sem, (t, q), mate))
            next(gram_w)
        x_arrivals = later
        transpose_into(t, same, core)
        for copy in mate_copies:
            copy.wait_recv()
        transpose_into(t, source * CORES + 1 - core, 1 - core)
        product_tiles(t, source)
    w_store = pltpu.make_async_copy(w_full, w_out, out_sem.at[0])
    w_store.start()

    for _ in ring_reduce(prod, 0, qb, ring_a, ring_b, ring_sem):
        next(gram_w, None)
    for _ in gram_w:
        pass

    own_h = rows_at(samp * qb, qb)
    sweep(h_full.at[own_h], prod.at[own_h], 1)
    for _ in ring_gather(h_full, 0, qb, back_sem):
        pass
    h_store = pltpu.make_async_copy(h_full, h_out, out_sem.at[1])
    h_store.start()
    for copy in sent:
        copy.wait_send()
    w_store.wait()
    h_store.wait()


def shards(n_samp, n_col, spectra, w_start, h_start):
    rows, rank = w_start.shape
    cols = h_start.shape[0]
    chips = n_col // CORES
    rb, qb, gb = rows // n_col, cols // n_samp, rank // 2 // n_samp
    dma = pltpu.SemaphoreType.DMA
    hops = n_samp - 1
    scratch = [
        pltpu.VMEM((rows, cols), F32),
        pltpu.VMEM((rows, rank), F32),
        pltpu.VMEM((cols, rank), F32),
        pltpu.VMEM((cols, rank), BF16),
        pltpu.VMEM((cols, rank), BF16),
        pltpu.VMEM((chips, rank, CORES * rb), BF16),
        pltpu.VMEM((chips, rank, CORES * rb), BF16),
        pltpu.VMEM((rank, cols), F32),
        pltpu.VMEM((max(rows, cols), rank), F32),
        pltpu.VMEM((chips, rb, rank), F32),
        pltpu.VMEM((chips - 1, rb, rank), F32),
        pltpu.VMEM((hops, qb // 2, rank), F32),
        pltpu.VMEM((hops, qb // 2, rank), F32),
        pltpu.VMEM((2, rank, rank), F32),
        pltpu.VMEM((2, rank // 2, rank), F32),
        pltpu.VMEM((2, hops, gb // 2, rank), F32),
        pltpu.VMEM((2, hops, gb // 2, rank), F32),
        pltpu.VMEM((2, chips - 1, gb, rank), F32),
        pltpu.VMEM((2, rank, rank), F32),
        pltpu.VMEM((rank // BLOCK, rank, 2 * BLOCK), BF16),
        pltpu.VMEM((max(rb, qb), rank), BF16),
        pltpu.VMEM((max(rb, qb), rank), BF16),
        dma((2 + 2 * chips,)),
        dma((2, chips)),
        dma((2, chips)),
        dma((2, chips, PIECES)),
        dma((2, chips, PIECES)),
        dma((2, 2, n_samp)),
        dma((2, 2, n_samp)),
        dma((2, 2)),
        dma((2, 2, 2, n_samp)),
        dma((2, 2, chips)),
        dma((2, 2, 2, n_samp)),
        dma((2, 2)),
        dma((2,)),
    ]
    return pl.pallas_call(
        functools.partial(kernel, n_samp, n_col),
        out_shape=(
            jax.ShapeDtypeStruct((rows, rank), F32),
            jax.ShapeDtypeStruct((cols, rank), F32),
        ),
        in_specs=[pl.BlockSpec(memory_space=pl.ANY)] * 3,
        out_specs=[pl.BlockSpec(memory_space=pl.ANY)] * 2,
        scratch_shapes=scratch,
        compiler_params=pltpu.CompilerParams(
            collective_id=0, has_side_effects=True, vmem_limit_bytes=63 * 1024 * 1024
        ),
    )(spectra, w_start, h_start)


def solution(mesh):
    return jax.shard_map(
        functools.partial(shards, mesh.shape["samp"], mesh.shape["col"]),
        mesh=mesh,
        in_specs=(P("samp", "col"), P("samp", None), P("col", None)),
        out_specs=(P("samp", None), P("col", None)),
        check_vma=False,
    )
```

```python
import functools

import jax
import jax.numpy as jnp
from jax import lax
from jax.experimental import pallas as pl
from jax.experimental.pallas import tpu as pltpu
from jax.sharding import PartitionSpec as P

BLOCK = 128
SWEEPS = 3
FLOOR = 1e-06
MESH = pl.DeviceIdType.MESH
F32 = jnp.float32
BF16 = jnp.bfloat16
CORES = 2
DEPTH = 4
PIECES = 4
HALVES = 2
CHAINS = 4
TILE = 256


def split(x):
    high = x.astype(BF16)
    return high, (x - high.astype(F32)).astype(BF16)


def dot(a, b):
    return jnp.dot(a, b, preferred_element_type=F32)


def dot3(ah, al, bh, bl):
    return dot(ah, bh) + (dot(ah, bl) + dot(al, bh))


def kernel(
    n_samp, n_col, spectra, w_start, h_start, w_out, h_out,
    spec, w_full, h_full, hh, hl, wth, wtl, pt, prod, acc, xrecv, ring_a, ring_b,
    gp, gcore, gring, gx, gram, gcat, fh, fl,
    load_sem, core_sem, x_sem, ag_sem, fwd_sem, ring_sem, back_sem,
    gcore_sem, gring_sem, gx_sem, gback_sem, gout_sem, out_sem,
):
    rows, rank = w_full.shape
    cols = h_full.shape[0]
    chips = n_col // CORES
    rb = rows // n_col
    qb = cols // n_samp
    half_rank = rank // 2
    gb = half_rank // n_samp

    samp = lax.axis_index("samp")
    col = lax.axis_index("col")
    core = lax.rem(col, CORES)
    chip = col // CORES
    mate = {"col": chip * CORES + 1 - core}
    x_right = {"col": lax.rem(chip + 1, chips) * CORES + core}
    x_left = {"col": lax.rem(chip + chips - 1, chips) * CORES + core}
    width = n_samp // DEPTH
    z, y = samp // width, lax.rem(samp, width)
    pos = y * DEPTH + z + lax.rem(y, 2) * (DEPTH - 1 - 2 * z)

    def member(p):
        p = lax.rem(p + 2 * n_samp, n_samp)
        py, pr = p // DEPTH, lax.rem(p, DEPTH)
        pz = pr + lax.rem(py, 2) * (DEPTH - 1 - 2 * pr)
        return pz * width + py

    ring_next = {"samp": member(pos + 1)}
    ring_prev = {"samp": member(pos - 1)}

    def rows_at(start, size):
        return pl.ds(pl.multiple_of(start, size), size)

    def remote(src, dst, sems, index, device):
        return pltpu.make_async_remote_copy(
            src_ref=src, dst_ref=dst, send_sem=sems.at[(0,) + index], recv_sem=sems.at[(1,) + index],
            device_id=device, device_id_type=MESH,
        )

    sent = []

    def send(*args):
        copy = remote(*args)
        copy.start()
        sent.append(copy)
        return copy

    h_load = pltpu.make_async_copy(h_start, h_full, load_sem.at[0])
    h_load.start()
    order = []
    for t in range(chips):
        dest = lax.rem(chip - 1 - t + 2 * chips, chips)
        order.append((dest, dest * CORES + 1 - core, dest * CORES + core))
    spec_loads = []
    for t, (_, first, second) in enumerate(order):
        for u, blk in enumerate((first, second)):
            copy = pltpu.make_async_copy(
                spectra.at[rows_at(blk * rb, rb)], spec.at[rows_at(blk * rb, rb)], load_sem.at[2 + 2 * t + u]
            )
            copy.start()
            spec_loads.append(copy)
    own_w = rows_at(col * rb, rb)
    w_load = pltpu.make_async_copy(w_start.at[own_w], w_full.at[own_w], load_sem.at[1])
    w_load.start()

    barrier = pltpu.get_barrier_semaphore()
    greet = [mate, x_right, x_left]
    greet += [{"samp": lax.rem(samp + o, n_samp)} for o in range(1, n_samp)]
    for device in greet:
        pl.semaphore_signal(barrier, inc=1, device_id=device, device_id_type=MESH)
    pl.semaphore_wait(barrier, len(greet))

    part = qb // 2 // CHAINS
    lines = [(way, q) for q in range(CHAINS) for way in (0, 1)]

    def ring_rows(sign, away, way, q):
        owner = member(pos - sign * away)
        return rows_at(owner * qb + (way * CHAINS + q) * part, part)

    def ring_reduce(data, prepare):
        last = {}
        for t in range(n_samp):
            prepare(t)
            for way, q in lines:
                recv, device, sign = ((ring_a, ring_next, 1), (ring_b, ring_prev, -1))[way]
                where = ring_rows(sign, 1 + t, way, q)
                if t > 0:
                    last[way, q].wait_recv()
                    data[where] += recv[t - 1, q * part : (q + 1) * part]
                if t < n_samp - 1:
                    slot = recv.at[t, pl.ds(q * part, part)]
                    last[way, q] = send(data.at[where], slot, ring_sem, (way, t, q), device)
            yield

    def ring_gather(data):
        last = {}
        for t in range(n_samp):
            for way, q in lines:
                device, sign = ((ring_next, 1), (ring_prev, -1))[way]
                where = ring_rows(sign, t, way, q)
                if t > 0:
                    last[way, q].wait_recv()
                if t < n_samp - 1:
                    last[way, q] = send(data.at[where], data.at[where], back_sem, (way, t, q), device)

    def gram_sum(i):
        mine = core * half_rank
        other = (1 - core) * half_rank
        copy = send(gp.at[i, rows_at(other, half_rank)], gcore.at[i], gcore_sem, (i,), mate)
        yield
        copy.wait_recv()
        gp[i, rows_at(mine, half_rank)] += gcore[i]
        copies = []
        for o in range(1, n_samp):
            peer = lax.rem(samp + o, n_samp)
            block = gp.at[i, rows_at(mine + peer * gb, gb)]
            copies.append(send(block, gring.at[i, o - 1], gring_sem, (i, o - 1), {"samp": peer}))
        yield
        own = rows_at(mine + samp * gb, gb)
        total = gp[i, own]
        for o in range(1, n_samp):
            copies[o - 1].wait_recv()
            total = total + gring[i, o - 1]
        gp[i, own] = total
        for t in range(chips - 1):
            source = gp.at[i, own] if t == 0 else gx.at[i, t - 1]
            copy = send(source, gx.at[i, t], gx_sem, (i, t), x_right)
            yield
            copy.wait_recv()
            total = total + gx[i, t]
        gram[i, own] = total
        copies = []
        for o in range(1, n_samp):
            peer = lax.rem(samp + o, n_samp)
            copies.append(send(gram.at[i, own], gram.at[i, own], gback_sem, (i, o - 1), {"samp": peer}))
        yield
        for copy in copies:
            copy.wait_recv()
        where = rows_at(mine, half_rank)
        copy = send(gram.at[i, where], gram.at[i, where], gout_sem, (i,), mate)
        yield
        copy.wait_recv()

    def sweep_scale(g):
        scale = []
        for b in range(rank // BLOCK):
            cols_b = slice(b * BLOCK, (b + 1) * BLOCK)
            high, low = split(gram[g, :, cols_b])
            gcat[b, :, :BLOCK] = high
            gcat[b, :, BLOCK:] = low
            scale.append(1.0 / jnp.sum(gram[g, cols_b, cols_b], axis=0, keepdims=True))
        return scale

    def sweep(factor, product, scale):
        n = factor.shape[0]
        for b in range(rank // BLOCK):
            cols_b = slice(b * BLOCK, (b + 1) * BLOCK)
            high, low = split(factor[:, cols_b])
            fh[:n, cols_b] = high
            fl[:n, cols_b] = low

        def one(_, carry):
            for b in range(rank // BLOCK):
                cols_b = slice(b * BLOCK, (b + 1) * BLOCK)
                both = dot(fh[:n], gcat[b])
                low = dot(fl[:n], gcat[b, :, :BLOCK])
                fg = both[:, :BLOCK] + (both[:, BLOCK:] + low)
                block = jnp.maximum(factor[:, cols_b] + (product[:, cols_b] - fg) * scale[b], FLOOR)
                factor[:, cols_b] = block
                high, low = split(block)
                fh[:n, cols_b] = high
                fl[:n, cols_b] = low
            return carry

        lax.fori_loop(0, SWEEPS, one, 0)

    h_load.wait()
    share = h_full[rows_at(samp * qb, qb)]
    th, tl = split(share.T)
    bh, bl = split(share)
    gp[0] = dot3(th, tl, bh, bl)
    gram_h = gram_sum(0)
    next(gram_h)

    def split_h(i, carry):
        where = rows_at(i * TILE, TILE)
        hh[where], hl[where] = split(h_full[where])
        return carry

    lax.fori_loop(0, cols // TILE, split_h, 0)

    tile = rb // HALVES

    def product_rows(blk, u):
        sh, sl = split(spec[rows_at(blk * rb + u * tile, tile)])
        return dot3(sh, sl, hh[...], hl[...])

    x_copies = {}
    for t, (_, first, second) in enumerate(order):
        for u in range(HALVES):
            piece_rows = pl.ds(u * tile, tile)
            outgoing = prod.at[pl.ds(t * rb + u * tile, tile)]
            incoming = prod.at[pl.ds((chips + t) * rb + u * tile, tile)]
            if u == 0:
                spec_loads[2 * t].wait()
            outgoing[...] = product_rows(first, u)
            core_copy = send(outgoing, incoming, core_sem, (t, u), mate)
            if u == 0:
                spec_loads[2 * t + 1].wait()
            acc[t, piece_rows] = product_rows(second, u)
            core_copy.wait_recv()
            acc[t, piece_rows] += incoming[...]
            if t < chips - 1:
                if t > 0:
                    x_copies[t - 1, u].wait_recv()
                    acc[t, piece_rows] += xrecv[t - 1, piece_rows]
                x_copies[t, u] = send(acc.at[t, piece_rows], xrecv.at[t, piece_rows], x_sem, (t, u), x_right)
            next(gram_h, None)
    for _ in gram_h:
        pass
    early = list(sent)
    sent.clear()

    piece = rb // PIECES
    each = PIECES // HALVES

    def w_piece(block, q):
        return w_full.at[rows_at(block * rb + q * piece, piece)]

    w_load.wait()
    scale = sweep_scale(0)
    x_arrivals, mate_arrivals = [], []
    for u in range(HALVES):
        piece_rows = pl.ds(u * tile, tile)
        x_copies[chips - 2, u].wait_recv()
        acc[chips - 1, piece_rows] += xrecv[chips - 2, piece_rows]
        sweep(w_full.at[rows_at(col * rb + u * tile, tile)], acc.at[chips - 1, piece_rows], scale)
        for q in range(u * each, (u + 1) * each):
            x_arrivals.append(send(w_piece(col, q), w_piece(col, q), ag_sem, (0, q), x_right))
            mate_arrivals.append(send(w_piece(col, q), w_piece(col, q), fwd_sem, (0, q), mate))

    def transpose_into(t, block, half):
        step = min(TILE, rb)
        for i in range(rb // step):
            high, low = split(w_full[rows_at(block * rb + i * step, step)].T)
            where = rows_at(half * rb + i * step, step)
            wth[t, :, where] = high
            wtl[t, :, where] = low

    transpose_into(0, col, core)
    lanes = rows_at(core * rb, rb)
    bh, bl = split(w_full[own_w])
    gp[1] = dot3(wth[0, :, lanes], wtl[0, :, lanes], bh, bl)
    gram_w = gram_sum(1)
    next(gram_w)
    for copy in mate_arrivals:
        copy.wait_recv()
    transpose_into(0, chip * CORES + 1 - core, 1 - core)
    next(gram_w)

    def product_tile(t, source, start, size):
        span = CORES * rb
        lane = rows_at(start, size)
        sh, sl = split(spec[rows_at(source * span, span), lane])
        partial = dot3(wth[t], wtl[t], sh, sl)
        if t > 0:
            partial = partial + pt[:, lane]
        if t == chips - 1:
            prod[lane] = partial.T
        else:
            pt[:, lane] = partial

    def product_tiles(t, source):
        def body(i, carry):
            product_tile(t, source, i * TILE, TILE)
            return carry

        lax.fori_loop(0, cols // TILE, body, 0)

    for copy in early:
        copy.wait_send()
    product_tiles(0, chip)
    for t in range(1, chips):
        source = lax.rem(chip - t + chips, chips)
        same = source * CORES + core
        later, mate_copies = [], []
        for q in range(PIECES):
            x_arrivals[q].wait_recv()
            if t < chips - 1:
                later.append(send(w_piece(same, q), w_piece(same, q), ag_sem, (t, q), x_right))
            mate_copies.append(send(w_piece(same, q), w_piece(same, q), fwd_sem, (t, q), mate))
            next(gram_w, None)
        x_arrivals = later
        transpose_into(t, same, core)
        for copy in mate_copies:
            copy.wait_recv()
        transpose_into(t, source * CORES + 1 - core, 1 - core)
        if t < chips - 1 or qb % BLOCK:
            product_tiles(t, source)
    w_store = pltpu.make_async_copy(w_full, w_out, out_sem.at[0])
    w_store.start()

    source = lax.rem(chip + 1, chips)

    def prepare(t):
        if qb % BLOCK:
            return

        def body(i, carry):
            product_tile(chips - 1, source, member(pos + (1 - 2 * i) * (1 + t)) * qb, qb)
            return carry

        if t < n_samp // 2 - 1:
            lax.fori_loop(0, 2, body, 0)
        elif t == n_samp // 2 - 1:
            product_tile(chips - 1, source, member(pos + n_samp // 2) * qb, qb)
        elif t == n_samp // 2:
            product_tile(chips - 1, source, samp * qb, qb)

    for t, _ in enumerate(ring_reduce(prod, prepare)):
        if t >= n_samp // 2:
            next(gram_w, None)
    for _ in gram_w:
        pass

    own_h = rows_at(samp * qb, qb)
    sweep(h_full.at[own_h], prod.at[own_h], sweep_scale(1))
    ring_gather(h_full)
    h_store = pltpu.make_async_copy(h_full, h_out, out_sem.at[1])
    h_store.start()
    for copy in sent:
        copy.wait_send()
    w_store.wait()
    h_store.wait()


def shards(n_samp, n_col, spectra, w_start, h_start):
    rows, rank = w_start.shape
    cols = h_start.shape[0]
    chips = n_col // CORES
    rb, qb, gb = rows // n_col, cols // n_samp, rank // 2 // n_samp
    dma = pltpu.SemaphoreType.DMA
    hops = n_samp - 1
    scratch = [
        pltpu.VMEM((rows, cols), F32),
        pltpu.VMEM((rows, rank), F32),
        pltpu.VMEM((cols, rank), F32),
        pltpu.VMEM((cols, rank), BF16),
        pltpu.VMEM((cols, rank), BF16),
        pltpu.VMEM((chips, rank, CORES * rb), BF16),
        pltpu.VMEM((chips, rank, CORES * rb), BF16),
        pltpu.VMEM((rank, cols), F32),
        pltpu.VMEM((max(rows, cols), rank), F32),
        pltpu.VMEM((chips, rb, rank), F32),
        pltpu.VMEM((chips - 1, rb, rank), F32),
        pltpu.VMEM((hops, qb // 2, rank), F32),
        pltpu.VMEM((hops, qb // 2, rank), F32),
        pltpu.VMEM((2, rank, rank), F32),
        pltpu.VMEM((2, rank // 2, rank), F32),
        pltpu.VMEM((2, hops, gb, rank), F32),
        pltpu.VMEM((2, chips - 1, gb, rank), F32),
        pltpu.VMEM((2, rank, rank), F32),
        pltpu.VMEM((rank // BLOCK, rank, 2 * BLOCK), BF16),
        pltpu.VMEM((max(rb, qb), rank), BF16),
        pltpu.VMEM((max(rb, qb), rank), BF16),
        dma((2 + 2 * chips,)),
        dma((2, chips, HALVES)),
        dma((2, chips, HALVES)),
        dma((2, chips, PIECES)),
        dma((2, chips, PIECES)),
        dma((2, 2, n_samp, CHAINS)),
        dma((2, 2, n_samp, CHAINS)),
        dma((2, 2)),
        dma((2, 2, n_samp)),
        dma((2, 2, chips)),
        dma((2, 2, n_samp)),
        dma((2, 2)),
        dma((2,)),
    ]
    return pl.pallas_call(
        functools.partial(kernel, n_samp, n_col),
        out_shape=(
            jax.ShapeDtypeStruct((rows, rank), F32),
            jax.ShapeDtypeStruct((cols, rank), F32),
        ),
        in_specs=[pl.BlockSpec(memory_space=pl.ANY)] * 3,
        out_specs=[pl.BlockSpec(memory_space=pl.ANY)] * 2,
        scratch_shapes=scratch,
        compiler_params=pltpu.CompilerParams(
            collective_id=0, has_side_effects=True, vmem_limit_bytes=63 * 1024 * 1024
        ),
    )(spectra, w_start, h_start)


def solution(mesh):
    return jax.shard_map(
        functools.partial(shards, mesh.shape["samp"], mesh.shape["col"]),
        mesh=mesh,
        in_specs=(P("samp", "col"), P("samp", None), P("col", None)),
        out_specs=(P("samp", None), P("col", None)),
        check_vma=False,
    )
```

```python
import functools

import jax
import jax.numpy as jnp
from jax import lax
from jax.experimental import pallas as pl
from jax.experimental.pallas import tpu as pltpu
from jax.sharding import PartitionSpec as P

BLOCK = 128
SWEEPS = 3
FLOOR = 1e-06
MESH = pl.DeviceIdType.MESH
F32 = jnp.float32
BF16 = jnp.bfloat16
CORES = 2
DEPTH = 4
PIECES = 4
HALVES = 2
CHAINS = 2
TILE = 256


def split(x):
    high = x.astype(BF16)
    return high, (x - high.astype(F32)).astype(BF16)


def dot(a, b):
    return jnp.dot(a, b, preferred_element_type=F32)


def dot3(ah, al, bh, bl):
    return dot(ah, bh) + (dot(ah, bl) + dot(al, bh))


def kernel(
    n_samp, n_col, spectra, w_start, h_start, w_out, h_out,
    spec, w_full, h_full, hh, hl, wth, wtl, pt, prod, acc, xrecv, ring_a, ring_b,
    gp, gcore, gring, gx, gram, gcat, fh, fl,
    load_sem, core_sem, x_sem, ag_sem, fwd_sem, ring_sem, back_sem,
    gcore_sem, gring_sem, gx_sem, gback_sem, gout_sem, out_sem,
):
    rows, rank = w_full.shape
    cols = h_full.shape[0]
    chips = n_col // CORES
    rb = rows // n_col
    qb = cols // n_samp
    half_rank = rank // 2
    gb = half_rank // n_samp

    samp = lax.axis_index("samp")
    col = lax.axis_index("col")
    core = lax.rem(col, CORES)
    chip = col // CORES
    mate = {"col": chip * CORES + 1 - core}
    x_right = {"col": lax.rem(chip + 1, chips) * CORES + core}
    x_left = {"col": lax.rem(chip + chips - 1, chips) * CORES + core}
    width = n_samp // DEPTH
    z, y = samp // width, lax.rem(samp, width)
    pos = y * DEPTH + z + lax.rem(y, 2) * (DEPTH - 1 - 2 * z)

    def member(p):
        p = lax.rem(p + 2 * n_samp, n_samp)
        py, pr = p // DEPTH, lax.rem(p, DEPTH)
        pz = pr + lax.rem(py, 2) * (DEPTH - 1 - 2 * pr)
        return pz * width + py

    ring_next = {"samp": member(pos + 1)}
    ring_prev = {"samp": member(pos - 1)}

    def rows_at(start, size):
        return pl.ds(pl.multiple_of(start, size), size)

    def remote(src, dst, sems, index, device):
        return pltpu.make_async_remote_copy(
            src_ref=src, dst_ref=dst, send_sem=sems.at[(0,) + index], recv_sem=sems.at[(1,) + index],
            device_id=device, device_id_type=MESH,
        )

    sent = []

    def send(*args):
        copy = remote(*args)
        copy.start()
        sent.append(copy)
        return copy

    h_load = pltpu.make_async_copy(h_start, h_full, load_sem.at[0])
    h_load.start()
    order = []
    for t in range(chips):
        dest = lax.rem(chip - 1 - t + 2 * chips, chips)
        order.append((dest, dest * CORES + 1 - core, dest * CORES + core))
    spec_loads = []
    for t, (_, first, second) in enumerate(order):
        for u, blk in enumerate((first, second)):
            copy = pltpu.make_async_copy(
                spectra.at[rows_at(blk * rb, rb)], spec.at[rows_at(blk * rb, rb)], load_sem.at[2 + 2 * t + u]
            )
            copy.start()
            spec_loads.append(copy)
    own_w = rows_at(col * rb, rb)
    w_load = pltpu.make_async_copy(w_start.at[own_w], w_full.at[own_w], load_sem.at[1])
    w_load.start()

    barrier = pltpu.get_barrier_semaphore()
    greet = [mate, x_right, x_left]
    greet += [{"samp": lax.rem(samp + o, n_samp)} for o in range(1, n_samp)]
    for device in greet:
        pl.semaphore_signal(barrier, inc=1, device_id=device, device_id_type=MESH)
    pl.semaphore_wait(barrier, len(greet))

    part = qb // 2 // CHAINS
    lines = [(way, q) for q in range(CHAINS) for way in (0, 1)]

    def ring_rows(sign, away, way, q):
        owner = member(pos - sign * away)
        return rows_at(owner * qb + (way * CHAINS + q) * part, part)

    def ring_reduce(data, prepare):
        last = {}
        for t in range(n_samp):
            prepare(t)
            for way, q in lines:
                recv, device, sign = ((ring_a, ring_next, 1), (ring_b, ring_prev, -1))[way]
                where = ring_rows(sign, 1 + t, way, q)
                if t > 0:
                    last[way, q].wait_recv()
                    data[where] += recv[t - 1, q * part : (q + 1) * part]
                if t < n_samp - 1:
                    slot = recv.at[t, pl.ds(q * part, part)]
                    last[way, q] = send(data.at[where], slot, ring_sem, (way, t, q), device)
            yield

    def ring_gather(data):
        last = {}
        for t in range(n_samp):
            for way, q in lines:
                device, sign = ((ring_next, 1), (ring_prev, -1))[way]
                where = ring_rows(sign, t, way, q)
                if t > 0:
                    last[way, q].wait_recv()
                if t < n_samp - 1:
                    last[way, q] = send(data.at[where], data.at[where], back_sem, (way, t, q), device)

    def gram_sum(i):
        mine = core * half_rank
        other = (1 - core) * half_rank
        copy = send(gp.at[i, rows_at(other, half_rank)], gcore.at[i], gcore_sem, (i,), mate)
        yield
        copy.wait_recv()
        gp[i, rows_at(mine, half_rank)] += gcore[i]
        copies = []
        for o in range(1, n_samp):
            peer = lax.rem(samp + o, n_samp)
            block = gp.at[i, rows_at(mine + peer * gb, gb)]
            copies.append(send(block, gring.at[i, o - 1], gring_sem, (i, o - 1), {"samp": peer}))
        yield
        own = rows_at(mine + samp * gb, gb)
        total = gp[i, own]
        for o in range(1, n_samp):
            copies[o - 1].wait_recv()
            total = total + gring[i, o - 1]
        gp[i, own] = total
        for t in range(chips - 1):
            source = gp.at[i, own] if t == 0 else gx.at[i, t - 1]
            copy = send(source, gx.at[i, t], gx_sem, (i, t), x_right)
            yield
            copy.wait_recv()
            total = total + gx[i, t]
        gram[i, own] = total
        copies = []
        for o in range(1, n_samp):
            peer = lax.rem(samp + o, n_samp)
            copies.append(send(gram.at[i, own], gram.at[i, own], gback_sem, (i, o - 1), {"samp": peer}))
        yield
        for copy in copies:
            copy.wait_recv()
        where = rows_at(mine, half_rank)
        copy = send(gram.at[i, where], gram.at[i, where], gout_sem, (i,), mate)
        yield
        copy.wait_recv()

    def sweep_scale(g):
        scale = []
        for b in range(rank // BLOCK):
            cols_b = slice(b * BLOCK, (b + 1) * BLOCK)
            high, low = split(gram[g, :, cols_b])
            gcat[b, :, :BLOCK] = high
            gcat[b, :, BLOCK:] = low
            scale.append(1.0 / jnp.sum(gram[g, cols_b, cols_b], axis=0, keepdims=True))
        return scale

    def sweep(factor, product, scale):
        n = factor.shape[0]
        for b in range(rank // BLOCK):
            cols_b = slice(b * BLOCK, (b + 1) * BLOCK)
            high, low = split(factor[:, cols_b])
            fh[:n, cols_b] = high
            fl[:n, cols_b] = low

        def one(_, carry):
            for b in range(rank // BLOCK):
                cols_b = slice(b * BLOCK, (b + 1) * BLOCK)
                both = dot(fh[:n], gcat[b])
                low = dot(fl[:n], gcat[b, :, :BLOCK])
                fg = both[:, :BLOCK] + (both[:, BLOCK:] + low)
                block = jnp.maximum(factor[:, cols_b] + (product[:, cols_b] - fg) * scale[b], FLOOR)
                factor[:, cols_b] = block
                high, low = split(block)
                fh[:n, cols_b] = high
                fl[:n, cols_b] = low
            return carry

        lax.fori_loop(0, SWEEPS, one, 0)

    h_load.wait()
    share = h_full[rows_at(samp * qb, qb)]
    th, tl = split(share.T)
    bh, bl = split(share)
    gp[0] = dot3(th, tl, bh, bl)
    gram_h = gram_sum(0)
    next(gram_h)

    def split_h(i, carry):
        where = rows_at(i * TILE, TILE)
        hh[where], hl[where] = split(h_full[where])
        return carry

    lax.fori_loop(0, cols // TILE, split_h, 0)

    tile = rb // HALVES

    def product_rows(blk, u):
        sh, sl = split(spec[rows_at(blk * rb + u * tile, tile)])
        return dot3(sh, sl, hh[...], hl[...])

    x_copies = {}
    for t, (_, first, second) in enumerate(order):
        for u in range(HALVES):
            piece_rows = pl.ds(u * tile, tile)
            outgoing = prod.at[pl.ds(t * rb + u * tile, tile)]
            incoming = prod.at[pl.ds((chips + t) * rb + u * tile, tile)]
            if u == 0:
                spec_loads[2 * t].wait()
            outgoing[...] = product_rows(first, u)
            core_copy = send(outgoing, incoming, core_sem, (t, u), mate)
            if u == 0:
                spec_loads[2 * t + 1].wait()
            acc[t, piece_rows] = product_rows(second, u)
            core_copy.wait_recv()
            acc[t, piece_rows] += incoming[...]
            if t < chips - 1:
                if t > 0:
                    x_copies[t - 1, u].wait_recv()
                    acc[t, piece_rows] += xrecv[t - 1, piece_rows]
                x_copies[t, u] = send(acc.at[t, piece_rows], xrecv.at[t, piece_rows], x_sem, (t, u), x_right)
            next(gram_h, None)
    for _ in gram_h:
        pass
    early = list(sent)
    sent.clear()

    piece = rb // PIECES
    each = PIECES // HALVES

    def w_piece(block, q):
        return w_full.at[rows_at(block * rb + q * piece, piece)]

    w_load.wait()
    scale = sweep_scale(0)
    x_arrivals, mate_arrivals = [], []
    for u in range(HALVES):
        piece_rows = pl.ds(u * tile, tile)
        x_copies[chips - 2, u].wait_recv()
        acc[chips - 1, piece_rows] += xrecv[chips - 2, piece_rows]
        sweep(w_full.at[rows_at(col * rb + u * tile, tile)], acc.at[chips - 1, piece_rows], scale)
        for q in range(u * each, (u + 1) * each):
            x_arrivals.append(send(w_piece(col, q), w_piece(col, q), ag_sem, (0, q), x_right))
            mate_arrivals.append(send(w_piece(col, q), w_piece(col, q), fwd_sem, (0, q), mate))

    def transpose_into(t, block, half):
        step = min(TILE, rb)
        for i in range(rb // step):
            high, low = split(w_full[rows_at(block * rb + i * step, step)].T)
            where = rows_at(half * rb + i * step, step)
            wth[t, :, where] = high
            wtl[t, :, where] = low

    transpose_into(0, col, core)
    lanes = rows_at(core * rb, rb)
    bh, bl = split(w_full[own_w])
    gp[1] = dot3(wth[0, :, lanes], wtl[0, :, lanes], bh, bl)
    gram_w = gram_sum(1)
    next(gram_w)
    for copy in mate_arrivals:
        copy.wait_recv()
    transpose_into(0, chip * CORES + 1 - core, 1 - core)
    next(gram_w)

    def product_tile(t, source, start, size):
        span = CORES * rb
        lane = rows_at(start, size)
        sh, sl = split(spec[rows_at(source * span, span), lane])
        partial = dot3(wth[t], wtl[t], sh, sl)
        if t > 0:
            partial = partial + pt[:, lane]
        if t == chips - 1:
            prod[lane] = partial.T
        else:
            pt[:, lane] = partial

    def product_tiles(t, source):
        def body(i, carry):
            product_tile(t, source, i * TILE, TILE)
            return carry

        lax.fori_loop(0, cols // TILE, body, 0)

    for copy in early:
        copy.wait_send()
    product_tiles(0, chip)
    for t in range(1, chips):
        source = lax.rem(chip - t + chips, chips)
        same = source * CORES + core
        later, mate_copies = [], []
        for q in range(PIECES):
            x_arrivals[q].wait_recv()
            if t < chips - 1:
                later.append(send(w_piece(same, q), w_piece(same, q), ag_sem, (t, q), x_right))
            mate_copies.append(send(w_piece(same, q), w_piece(same, q), fwd_sem, (t, q), mate))
            next(gram_w, None)
        x_arrivals = later
        transpose_into(t, same, core)
        for copy in mate_copies:
            copy.wait_recv()
        transpose_into(t, source * CORES + 1 - core, 1 - core)
        if t < chips - 1 or qb % BLOCK:
            product_tiles(t, source)
    w_store = pltpu.make_async_copy(w_full, w_out, out_sem.at[0])
    w_store.start()

    source = lax.rem(chip + 1, chips)

    def prepare(t):
        if qb % BLOCK:
            return

        def body(i, carry):
            product_tile(chips - 1, source, member(pos + (1 - 2 * i) * (1 + t)) * qb, qb)
            return carry

        if t < n_samp // 2 - 1:
            lax.fori_loop(0, 2, body, 0)
        elif t == n_samp // 2 - 1:
            product_tile(chips - 1, source, member(pos + n_samp // 2) * qb, qb)
        elif t == n_samp // 2:
            product_tile(chips - 1, source, samp * qb, qb)

    for t, _ in enumerate(ring_reduce(prod, prepare)):
        if t >= n_samp // 2:
            next(gram_w, None)
    for _ in gram_w:
        pass

    own_h = rows_at(samp * qb, qb)
    sweep(h_full.at[own_h], prod.at[own_h], sweep_scale(1))
    ring_gather(h_full)
    h_store = pltpu.make_async_copy(h_full, h_out, out_sem.at[1])
    h_store.start()
    for copy in sent:
        copy.wait_send()
    w_store.wait()
    h_store.wait()


def shards(n_samp, n_col, spectra, w_start, h_start):
    rows, rank = w_start.shape
    cols = h_start.shape[0]
    chips = n_col // CORES
    rb, qb, gb = rows // n_col, cols // n_samp, rank // 2 // n_samp
    dma = pltpu.SemaphoreType.DMA
    hops = n_samp - 1
    scratch = [
        pltpu.VMEM((rows, cols), F32),
        pltpu.VMEM((rows, rank), F32),
        pltpu.VMEM((cols, rank), F32),
        pltpu.VMEM((cols, rank), BF16),
        pltpu.VMEM((cols, rank), BF16),
        pltpu.VMEM((chips, rank, CORES * rb), BF16),
        pltpu.VMEM((chips, rank, CORES * rb), BF16),
        pltpu.VMEM((rank, cols), F32),
        pltpu.VMEM((max(rows, cols), rank), F32),
        pltpu.VMEM((chips, rb, rank), F32),
        pltpu.VMEM((chips - 1, rb, rank), F32),
        pltpu.VMEM((hops, qb // 2, rank), F32),
        pltpu.VMEM((hops, qb // 2, rank), F32),
        pltpu.VMEM((2, rank, rank), F32),
        pltpu.VMEM((2, rank // 2, rank), F32),
        pltpu.VMEM((2, hops, gb, rank), F32),
        pltpu.VMEM((2, chips - 1, gb, rank), F32),
        pltpu.VMEM((2, rank, rank), F32),
        pltpu.VMEM((rank // BLOCK, rank, 2 * BLOCK), BF16),
        pltpu.VMEM((max(rb, qb), rank), BF16),
        pltpu.VMEM((max(rb, qb), rank), BF16),
        dma((2 + 2 * chips,)),
        dma((2, chips, HALVES)),
        dma((2, chips, HALVES)),
        dma((2, chips, PIECES)),
        dma((2, chips, PIECES)),
        dma((2, 2, n_samp, CHAINS)),
        dma((2, 2, n_samp, CHAINS)),
        dma((2, 2)),
        dma((2, 2, n_samp)),
        dma((2, 2, chips)),
        dma((2, 2, n_samp)),
        dma((2, 2)),
        dma((2,)),
    ]
    return pl.pallas_call(
        functools.partial(kernel, n_samp, n_col),
        out_shape=(
            jax.ShapeDtypeStruct((rows, rank), F32),
            jax.ShapeDtypeStruct((cols, rank), F32),
        ),
        in_specs=[pl.BlockSpec(memory_space=pl.ANY)] * 3,
        out_specs=[pl.BlockSpec(memory_space=pl.ANY)] * 2,
        scratch_shapes=scratch,
        compiler_params=pltpu.CompilerParams(
            collective_id=0, has_side_effects=True, vmem_limit_bytes=63 * 1024 * 1024
        ),
    )(spectra, w_start, h_start)


def solution(mesh):
    return jax.shard_map(
        functools.partial(shards, mesh.shape["samp"], mesh.shape["col"]),
        mesh=mesh,
        in_specs=(P("samp", "col"), P("samp", None), P("col", None)),
        out_specs=(P("samp", None), P("col", None)),
        check_vma=False,
    )
```
